512 devices in a mesh: grid: 64 (over z_hi, x, y), mem: 8 (over z_lo, core).
Axes of the slice: x: 4, y: 4, z: 16 (z_hi: 4, z_lo: 4; z = z_hi * 4 + z_lo), core: 2. Of those that a mesh axis runs over, the one named last changes fastest.
Arguments:
- queries: bfloat16 [8, 16384, 1024], P('mem', 'grid'), may hold values from -80 to 80
- keys: bfloat16 [8, 16384, 1024], P('mem', 'grid'), may hold values from -8 to 8
- values: bfloat16 [8, 16384, 1024], P('mem', 'grid'), may hold values from -6 to 6
- truth: bfloat16 [16384, 1024], P('grid'), may hold values from -2 to 2
- widths: int32 [16], replicated, may hold values from 1 to 2, as said below
- node_order: int32 [128], replicated, may hold values from 0 to 127, each once
Outputs:
- query_grads: bfloat16 [8, 16384, 1024], P('mem', 'grid')
- key_grads: bfloat16 [8, 16384, 1024], P('mem', 'grid')
- value_grads: bfloat16 [8, 16384, 1024], P('mem', 'grid')
The draws below stay inside these ranges and needn't reach their ends.
Inputs may be any that keep to these rules, and one draw needn't show every extreme that they name: `widths`: some head has half-width 2, some head 1.
All inputs are finite; a program needn't handle non-finite values.
Results may differ from the reference program's by a relative error of at most 0.0093.
Values may be sent and summed in bfloat16 or wider, within the bound.
A program may use at most 128 MiB of HBM per device.

```python
import jax
import jax.numpy as jnp
from jax import lax

D = 1024
HEADS = 16
BLOCK = 128
WMAX = 2
NODES = 16384
MEMBERS = 8


def clipped_base(key):
    return 1.6 * jnp.clip(jax.random.normal(jax.random.fold_in(key, 17), (MEMBERS, NODES, D), jnp.float32), -4.5, 4.5)


def draw_keys(key, part):
    base = clipped_base(key)
    return base.astype(jnp.bfloat16)


def draw_queries(key, part):
    base = clipped_base(key)
    key = jax.random.fold_in(key, 2)
    return (1.6 * jnp.clip(jax.random.normal(key, base.shape, jnp.float32), -4.5, 4.5)).astype(jnp.bfloat16)


def draw_widths(key, part):
    key = jax.random.fold_in(key, 3)
    widths = jax.random.randint(jax.random.fold_in(key, 1), (HEADS,), 1, WMAX + 1)
    first = jax.random.randint(jax.random.fold_in(key, 2), (), 0, HEADS)
    second = (first + jax.random.randint(jax.random.fold_in(key, 4), (), 1, HEADS)) % HEADS
    return widths.at[first].set(WMAX).at[second].set(1).astype(jnp.int32)


def block_levels(rng, dims, split, smallest, largest):
    level = 1.0
    for position, shards_of in split:
        steps = jax.random.uniform(jax.random.fold_in(jax.random.fold_in(rng, 6), position), (shards_of,), jnp.float32, smallest / len(split), largest / len(split))
        level = level * jnp.repeat(jnp.exp(steps), dims[position] // shards_of).reshape((-1,) + (1,) * (len(dims) - 1 - position))
    return level


def gaussian(stream_key, shape, spread, bound, cuts=(), kind=jnp.bfloat16):
    level = block_levels(stream_key, shape, cuts, -0.22, 0.18) if cuts else 1.0
    values = jax.random.normal(stream_key, shape, jnp.float32) * spread * level
    return jnp.minimum(jnp.maximum(values, -bound), bound).astype(kind)


def setup_inputs(seed: int = 0) -> dict:
    key_of = jax.random.split(jax.random.key(seed), 7)
    queries = draw_queries(jax.random.fold_in(key_of[6], 71), 0)
    keys = draw_keys(jax.random.fold_in(key_of[6], 71), 0)
    values = gaussian(key_of[2], (MEMBERS, NODES, D), 1.0, 6.0, ((0, 8), (1, 64)))
    truth = gaussian(key_of[3], (NODES, D), 0.3, 2.0, ((0, 64),))
    widths = draw_widths(jax.random.fold_in(key_of[6], 71), 0)
    node_order = jax.random.permutation(key_of[5], BLOCK).astype(jnp.int32)
    return {"queries": queries, "keys": keys, "values": values, "truth": truth, "widths": widths, "node_order": node_order}


NEG = -1e+30
SMOOTH = 0.25

def window_mask(query_count, key_count, query_shift, key_shift, block_size, widths):
    query_blocks = lax.broadcasted_iota(jnp.int32, (query_count, key_count), 0) // block_size - query_shift
    key_blocks = lax.broadcasted_iota(jnp.int32, (query_count, key_count), 1) // block_size - key_shift
    distance = jnp.abs(query_blocks - key_blocks)
    return distance[None, :, :] <= widths[:, None, None]

def smooth_slope(diff):
    return diff / jnp.sqrt(diff * diff + SMOOTH * SMOOTH)

def crps_grads(own_values, ensemble, target):
    own_f = own_values.astype(jnp.float32)
    total = jnp.zeros_like(own_f)
    members_count = ensemble.shape[0]
    for member in range(members_count):
        total = total + smooth_slope(own_f - ensemble[member].astype(jnp.float32))
    return (smooth_slope(own_f - target.astype(jnp.float32)) - total / (members_count - 1)).astype(jnp.bfloat16)

def reference(queries, keys, values, truth, widths, node_order):
    head_dim = D // HEADS
    score_scale = head_dim ** (-0.5)
    block_count = NODES // BLOCK
    reach = WMAX * BLOCK
    extended = BLOCK + 2 * reach
    offsets = jnp.arange(extended, dtype=jnp.int32) - reach
    allowed = window_mask(BLOCK, extended, 0, WMAX, BLOCK, widths)
    target = jnp.take(truth.reshape(block_count, BLOCK, D), node_order, axis=1).reshape(NODES, D)
    block_ids = jnp.arange(block_count, dtype=jnp.int32)

    def split_heads(rows_in):
        return rows_in.reshape(rows_in.shape[0], HEADS, head_dim).astype(jnp.float32)

    def masked_scores(query_b, key_b):
        scores = jnp.einsum('qhd,khd->hqk', query_b, key_b) * score_scale
        return jnp.where(allowed, scores, NEG)

    def forward_member(inputs):
        query_m, key_m, value_m = inputs

        def one_block(block_index):
            start = (block_index * BLOCK).astype(jnp.int32)
            index = (start + offsets) % NODES
            query_b = split_heads(lax.dynamic_slice_in_dim(query_m, start, BLOCK, 0))
            key_b = split_heads(jnp.take(key_m, index, axis=0))
            value_b = split_heads(jnp.take(value_m, index, axis=0))
            scores = masked_scores(query_b, key_b)
            highest = lax.optimization_barrier(jnp.max(scores, axis=2, keepdims=True))
            log_total = highest[:, :, 0] + jnp.log(lax.optimization_barrier(jnp.sum(jnp.exp(scores - highest), axis=2)))
            weights = jnp.exp(scores - log_total[:, :, None])
            rounded = lax.optimization_barrier(weights.astype(jnp.bfloat16)).astype(jnp.float32)
            mixed = jnp.einsum('hqk,khd->qhd', rounded, value_b).reshape(BLOCK, D).astype(jnp.bfloat16)
            return (mixed, log_total)
        mixed, totals = lax.map(one_block, block_ids)
        return (mixed.reshape(NODES, D), totals)
    outputs, totals = lax.map(forward_member, (queries, keys, values))

    def crps_block(block_index):
        start = (block_index * BLOCK).astype(jnp.int32)
        ensemble = lax.dynamic_slice_in_dim(outputs, start, BLOCK, 1)
        target_b = lax.dynamic_slice_in_dim(target, start, BLOCK, 0)
        return crps_grads(ensemble, ensemble, target_b)
    grads = lax.map(crps_block, block_ids)
    grads = jnp.transpose(grads, (1, 0, 2, 3)).reshape(outputs.shape)

    def backward_member(inputs):
        query_m, key_m, value_m, out_m, grad_m, totals_m = inputs

        def one_block(carry, block_index):
            key_acc, value_acc = carry
            start = (block_index * BLOCK).astype(jnp.int32)
            index = (start + offsets) % NODES
            query_b = split_heads(lax.dynamic_slice_in_dim(query_m, start, BLOCK, 0))
            grad_b = split_heads(lax.dynamic_slice_in_dim(grad_m, start, BLOCK, 0))
            out_b = split_heads(lax.dynamic_slice_in_dim(out_m, start, BLOCK, 0))
            key_b = split_heads(jnp.take(key_m, index, axis=0))
            value_b = split_heads(jnp.take(value_m, index, axis=0))
            inner = lax.optimization_barrier(jnp.sum(grad_b * out_b, axis=2)).T
            scores = masked_scores(query_b, key_b)
            log_total = lax.dynamic_index_in_dim(totals_m, block_index, 0, keepdims=False)
            weights = jnp.exp(scores - log_total[:, :, None])
            along = jnp.einsum('qhd,khd->hqk', grad_b, value_b)
            dscore = lax.optimization_barrier((weights * (along - inner[:, :, None])).astype(jnp.bfloat16)).astype(jnp.float32)
            query_grad = (jnp.einsum('hqk,khd->qhd', dscore, key_b) * score_scale).reshape(BLOCK, D).astype(jnp.bfloat16)
            key_part = jnp.einsum('hqk,qhd->khd', dscore, query_b) * score_scale
            rounded = lax.optimization_barrier(weights.astype(jnp.bfloat16)).astype(jnp.float32)
            value_part = jnp.einsum('hqk,qhd->khd', rounded, grad_b)
            key_acc = key_acc.at[index].add(key_part.reshape(extended, D))
            value_acc = value_acc.at[index].add(value_part.reshape(extended, D))
            return ((key_acc, value_acc), query_grad)
        zeros = jnp.zeros((NODES, D), jnp.float32)
        (key_acc, value_acc), query_grads = lax.scan(one_block, (zeros, zeros), block_ids)
        return (query_grads.reshape(NODES, D), key_acc.astype(jnp.bfloat16), value_acc.astype(jnp.bfloat16))
    query_grads, key_grads, value_grads = lax.map(backward_member, (queries, keys, values, outputs, grads, totals))
    return (query_grads, key_grads, value_grads)
```

```python
import functools

import jax
import jax.numpy as jnp
from jax import lax
from jax.experimental import pallas as pl
from jax.experimental.pallas import tpu as pltpu
from jax.sharding import PartitionSpec as P

HEAD = 64
BLOCK = 128
CHUNK = 2 * BLOCK
PLANE = 16
MEM = 8
UNITS = 4
NEG = -1e30
SMOOTH2 = 0.0625
MESH = pl.DeviceIdType.MESH

TN = (((0,), (0,)), ((), ()))
NT = (((1,), (1,)), ((), ()))
NN = (((1,), (0,)), ((), ()))


def dot(a, b, dims):
    return lax.dot_general(a, b, dims, preferred_element_type=jnp.float32)


def slope(diff):
    return diff * lax.rsqrt(diff * diff + SMOOTH2)


def kernel(
    widths, order, q_hbm, k_hbm, v_hbm, t_hbm,
    dq_out, dk_out, dv_out,
    q_in, k_in, v_in, t_in,
    stage, ext, tstage, tgt, weights, out_u, ens, gout, g_u, acc, back_low, back_high,
    dq_src, dkv_src, dq_dst, dkv_dst,
    load_sem, in_send, in_recv, t_send, t_recv, halo_send, halo_recv,
    m1_send, m1_recv, m2_send, m2_recv, back_send, back_recv,
    dq_send, dq_recv, dkv_send, dkv_recv,
):
    grid = lax.axis_index("grid")
    mem = lax.axis_index("mem")
    z_hi = grid // 16
    x = (grid // 4) % 4
    y = grid % 4
    p = grid % 16
    z_lo = mem // 2
    core = mem % 2

    def at_plane(xx, yy):
        return (z_hi * 16 + (xx % 4) * 4 + yy % 4, mem)

    def at_z(d):
        return (((z_hi + d) % 4) * 16 + p, mem)

    truth_from = (1 + z_lo) % 4
    sends_truth = y == truth_from
    loads = [
        pltpu.make_async_copy(src.at[0], dst, load_sem.at[i])
        for i, (src, dst) in enumerate(((q_hbm, q_in), (k_hbm, k_in), (v_hbm, v_in)))
    ]
    for load in loads:
        load.start()
    load_truth = pltpu.make_async_copy(
        t_hbm.at[pl.ds(pl.multiple_of(core * BLOCK, BLOCK), BLOCK)], t_in, load_sem.at[3]
    )
    load_truth.start()

    offsets = [(dx, dy) for dx in (0, 3, 2, 1) for dy in range(4)]
    barrier = pltpu.get_barrier_semaphore()
    for dx, dy in offsets[1:]:
        pl.semaphore_signal(barrier, inc=1, device_id=at_plane(x + dx, y + dy), device_id_type=MESH)
    for o in range(1, MEM):
        pl.semaphore_signal(barrier, inc=1, device_id=(grid, (mem + o) % MEM), device_id_type=MESH)
    for d in (1, 3):
        pl.semaphore_signal(barrier, inc=1, device_id=at_z(d), device_id_type=MESH)

    acc[...] = jnp.zeros_like(acc)
    for load in loads:
        load.wait()

    def to_stage(pair):
        lanes = pl.ds(pl.multiple_of(pair * 128, 128), 128)
        for i, ref in enumerate((q_in, k_in, v_in)):
            block = ref[:, lanes]
            if i == 0:
                block = block * jnp.bfloat16(0.125)
            block = block.T
            stage[pair * 2, pl.ds(i * HEAD, HEAD)] = block[:HEAD]
            stage[pair * 2 + 1, pl.ds(i * HEAD, HEAD)] = block[HEAD:]

    def in_copy(dx, dy):
        target = ((x + dx) % 4) * 4 + (y + dy) % 4
        return pltpu.make_async_remote_copy(
            src_ref=stage.at[target],
            dst_ref=ext.at[1 + p],
            send_sem=in_send.at[dx * 4 + dy],
            recv_sem=in_recv.at[dx * 4 + dy],
            device_id=at_plane(x + dx, y + dy),
            device_id_type=MESH,
        )

    first = True
    for dx in (0, 3, 2, 1):
        row = (x + dx) % 4
        to_stage(row * 2)
        to_stage(row * 2 + 1)
        if first:
            pl.semaphore_wait(barrier, 15 + 7 + 2)
            first = False
        for dy in (1, 3, 2, 0):
            if (dx, dy) != (0, 0):
                in_copy(dx, dy).start()
    ext[1 + p] = stage[p]

    load_truth.wait()

    def t_copy(dx, dy):
        return pltpu.make_async_remote_copy(
            src_ref=tstage.at[((x + dx) % 4) * 4 + (y + dy) % 4],
            dst_ref=tgt.at[dx],
            send_sem=t_send.at[dx * 4 + dy],
            recv_sem=t_recv.at[dx],
            device_id=at_plane(x + dx, y + dy),
            device_id_type=MESH,
        )

    @pl.when(sends_truth)
    def _():
        nodes = lax.broadcasted_iota(jnp.int32, (BLOCK, BLOCK), 0)
        pick = jnp.where(nodes == order[...], 1.0, 0.0).astype(jnp.bfloat16)
        for pair in range(8):
            ordered = dot(t_in[:, pair * 128 : pair * 128 + 128], pick, TN).astype(jnp.bfloat16)
            tstage[pair * 2] = ordered[:HEAD]
            tstage[pair * 2 + 1] = ordered[HEAD:]
        for dx, dy in offsets[1:]:
            t_copy(dx, dy).start()
        tgt[0] = tstage[p]

    far = jnp.where(widths[p] >= 2, 0.0, NEG).astype(jnp.float32)
    second = lax.broadcasted_iota(jnp.int32, (1, CHUNK), 1) >= BLOCK
    rows = lax.broadcasted_iota(jnp.int32, (CHUNK, 1), 0) >= BLOCK
    top_low, bottom_low = jnp.where(second, NEG, far), jnp.where(second, far, 0.0)
    top_high, bottom_high = jnp.where(second, 0.0, far), jnp.where(second, far, NEG)

    def halo_copy(up):
        src, dst = (PLANE, 0) if up else (1, PLANE + 1)
        i = 0 if up else 1
        return pltpu.make_async_remote_copy(
            src_ref=ext.at[src, pl.ds(HEAD, 2 * HEAD)],
            dst_ref=ext.at[dst, pl.ds(HEAD, 2 * HEAD)],
            send_sem=halo_send.at[i],
            recv_sem=halo_recv.at[i],
            device_id=at_z(1 if up else 3),
            device_id_type=MESH,
        )

    def wait_row(k):
        dx = (4 - k) % 4
        for dy in range(4):
            if (dx, dy) != (0, 0):
                in_copy(dx, dy).wait_recv()

        @pl.when((x + k) % 4 == 3)
        def _():
            halo_copy(True).start()

        @pl.when((x + k) % 4 == 0)
        def _():
            halo_copy(False).start()

    def m1_copy(k, o):
        return pltpu.make_async_remote_copy(
            src_ref=out_u.at[k, (mem + o) % MEM],
            dst_ref=ens.at[k, mem],
            send_sem=m1_send.at[k, o],
            recv_sem=m1_recv.at[k, o],
            device_id=(grid, (mem + o) % MEM),
            device_id_type=MESH,
        )

    def m2_copy(k, o):
        return pltpu.make_async_remote_copy(
            src_ref=gout.at[k, (mem + o) % MEM],
            dst_ref=g_u.at[k, mem],
            send_sem=m2_send.at[k, o],
            recv_sem=m2_recv.at[k, o],
            device_id=(grid, (mem + o) % MEM),
            device_id_type=MESH,
        )

    def chunk_of(k, i):
        return (((x + k) % 4) * 4 + 1 + i) % PLANE

    def forward(k):
        @pl.when((x + k) % 4 == 3)
        def _():
            halo_copy(True).wait_recv()
            halo_copy(False).wait_recv()

        def one(i, carry):
            j = chunk_of(k, i)
            q_t = ext[j + 1, pl.ds(0, HEAD)]
            scores = [dot(ext[j + t, pl.ds(HEAD, HEAD)], q_t, TN) for t in range(3)]
            scores[0] = scores[0] + jnp.where(rows, bottom_low, top_low)
            scores[2] = scores[2] + jnp.where(rows, bottom_high, top_high)
            highest = jnp.max(
                jnp.maximum(jnp.maximum(scores[0], scores[1]), scores[2]), axis=0, keepdims=True
            )
            terms = [jnp.exp(s - highest) for s in scores]
            total = jnp.sum(terms[0] + terms[1] + terms[2], axis=0, keepdims=True)
            share = 1.0 / total
            mixed = jnp.zeros((HEAD, CHUNK), jnp.float32)
            for t in range(3):
                low = (terms[t] * share).astype(jnp.bfloat16)
                weights[j, t] = low
                mixed = mixed + dot(ext[j + t, pl.ds(2 * HEAD, HEAD)], low, NN)
            mixed = mixed.astype(jnp.bfloat16)
            out_u[k, 2 * i] = mixed[:, :BLOCK]
            out_u[k, 2 * i + 1] = mixed[:, BLOCK:]
            return carry

        lax.fori_loop(0, 4, one, 0)
        for o in (1, 7, 2, 6, 3, 5, 4):
            m1_copy(k, o).start()
        ens[k, mem] = out_u[k, mem]

    def crps(k):
        dx = (8 - (z_lo // 3) - k) % 4
        if_remote = jnp.logical_not(sends_truth & (dx == 0))

        @pl.when(if_remote)
        def _():
            pltpu.make_async_remote_copy(
                src_ref=tstage.at[0],
                dst_ref=tgt.at[dx],
                send_sem=t_send.at[0],
                recv_sem=t_recv.at[dx],
                device_id=at_plane(x, y + 1),
                device_id_type=MESH,
            ).wait_recv()

        for o in range(1, MEM):
            m1_copy(k, o).wait_recv()
        own = [ens[k, n].astype(jnp.float32) for n in range(MEM)]
        target = tgt[dx].astype(jnp.float32)
        totals = [jnp.zeros((HEAD, BLOCK), jnp.float32) for _ in range(MEM)]
        for a in range(MEM):
            for b in range(a + 1, MEM):
                s = slope(own[a] - own[b])
                totals[a] = totals[a] + s
                totals[b] = totals[b] - s
        for n in range(MEM):
            gout[k, n] = (slope(own[n] - target) - totals[n] * (1.0 / (MEM - 1))).astype(jnp.bfloat16)
        for o in (1, 7, 2, 6, 3, 5, 4):
            m2_copy(k, o).start()
        g_u[k, mem] = gout[k, mem]

    def dq_copy(j):
        return pltpu.make_async_remote_copy(
            src_ref=dq_src.at[j],
            dst_ref=dq_dst.at[p],
            send_sem=dq_send.at[j],
            recv_sem=dq_recv.at[p],
            device_id=(z_hi * 16 + j, mem),
            device_id_type=MESH,
        )

    def dkv_copy(j):
        return pltpu.make_async_remote_copy(
            src_ref=dkv_src.at[j],
            dst_ref=dkv_dst.at[p],
            send_sem=dkv_send.at[j],
            recv_sem=dkv_recv.at[p],
            device_id=(z_hi * 16 + j, mem),
            device_id_type=MESH,
        )

    def send_dkv(j):
        @pl.when(j != p)
        def _():
            dkv_copy(j).start()

        @pl.when(j == p)
        def _():
            dkv_dst[p] = dkv_src[p]

    def back_copy(down):
        i = 0 if down else 1
        return pltpu.make_async_remote_copy(
            src_ref=dkv_src.at[PLANE + i],
            dst_ref=(back_high if down else back_low),
            send_sem=back_send.at[i],
            recv_sem=back_recv.at[i],
            device_id=at_z(3 if down else 1),
            device_id_type=MESH,
        )

    def finish_dkv(j):
        dkv_src[j] = acc[j + 1].astype(jnp.bfloat16)
        send_dkv(j)

    def backward(k):
        for o in range(1, MEM):
            m2_copy(k, o).wait_recv()

        def one(i, carry):
            j = chunk_of(k, i)
            q_t = ext[j + 1, pl.ds(0, HEAD)]
            g_t = jnp.concatenate([g_u[k, 2 * i], g_u[k, 2 * i + 1]], axis=1)
            o_t = jnp.concatenate([out_u[k, 2 * i], out_u[k, 2 * i + 1]], axis=1)
            inner = jnp.sum(g_t.astype(jnp.float32) * o_t.astype(jnp.float32), axis=0, keepdims=True)
            dq = jnp.zeros((HEAD, CHUNK), jnp.float32)
            for t in range(3):
                along = dot(ext[j + t, pl.ds(2 * HEAD, HEAD)], g_t, TN)
                low = weights[j, t]
                ds = (low.astype(jnp.float32) * (along - inner)).astype(jnp.bfloat16)
                dq = dq + dot(ext[j + t, pl.ds(HEAD, HEAD)], ds, NN)
                acc[j + t, pl.ds(0, HEAD)] += dot(q_t, ds, NT)
                acc[j + t, pl.ds(HEAD, HEAD)] += dot(g_t, low, NT)
            dq_src[j] = (dq * 0.125).astype(jnp.bfloat16)

            @pl.when(j != p)
            def _():
                dq_copy(j).start()

            @pl.when(j == p)
            def _():
                dq_dst[p] = dq_src[p]

            return carry

        lax.fori_loop(0, 4, one, 0)

        @pl.when((x + k) % 4 == 3)
        def _():
            dkv_src[PLANE] = acc[0].astype(jnp.bfloat16)
            back_copy(True).start()
            dkv_src[PLANE + 1] = acc[PLANE + 1].astype(jnp.bfloat16)
            back_copy(False).start()

        def done(i, carry):
            j = (((x + k) % 4) * 4 + i) % PLANE

            @pl.when((j != 0) & (j != PLANE - 1))
            def _():
                finish_dkv(j)

            return carry

        if k == 0:
            lax.fori_loop(2, 4, done, 0)
        elif k < UNITS - 1:
            lax.fori_loop(0, 4, done, 0)
        else:
            lax.fori_loop(0, 6, done, 0)

    wait_row(0)
    wait_row(1)
    forward(0)
    wait_row(2)
    forward(1)
    crps(0)
    wait_row(3)
    forward(2)
    crps(1)
    forward(3)
    backward(0)
    crps(2)
    backward(1)
    crps(3)
    backward(2)
    backward(3)

    back_copy(True).wait_recv()
    acc[PLANE] += back_high[...].astype(jnp.float32)
    finish_dkv(PLANE - 1)
    back_copy(False).wait_recv()
    acc[1] += back_low[...].astype(jnp.float32)
    finish_dkv(0)

    def arrived(n, recv):
        src = (p + n) % PLANE
        if recv is dq_recv:
            ref = dq_dst
        else:
            ref = dkv_dst
        pltpu.make_async_remote_copy(
            src_ref=ref.at[src], dst_ref=ref.at[src], send_sem=dq_send.at[0], recv_sem=recv.at[src],
            device_id=(z_hi * 16 + src, mem), device_id_type=MESH,
        ).wait_recv()

    def all_arrived(recv):
        def one(n, carry):
            arrived(n, recv)
            return carry

        lax.fori_loop(1, PLANE, one, 0)

    all_arrived(dq_recv)
    for pair in range(8):
        block = jnp.concatenate([dq_dst[2 * pair], dq_dst[2 * pair + 1]], axis=0)
        dq_out[0, :, pair * 128 : pair * 128 + 128] = block.T
    all_arrived(dkv_recv)
    for pair in range(8):
        for i, ref in enumerate((dk_out, dv_out)):
            block = jnp.concatenate(
                [dkv_dst[2 * pair, pl.ds(i * HEAD, HEAD)], dkv_dst[2 * pair + 1, pl.ds(i * HEAD, HEAD)]],
                axis=0,
            )
            ref[0, :, pair * 128 : pair * 128 + 128] = block.T

    for dx, dy in offsets[1:]:
        in_copy(dx, dy).wait_send()
    for up in (True, False):
        halo_copy(up).wait_send()
        back_copy(up).wait_send()
    for k in range(UNITS):
        for o in range(1, MEM):
            m1_copy(k, o).wait_send()
            m2_copy(k, o).wait_send()

    @pl.when(sends_truth)
    def _():
        for dx, dy in offsets[1:]:
            t_copy(dx, dy).wait_send()

    def sent(n, carry):
        j = (p + n) % PLANE
        dq_copy(j).wait_send()
        dkv_copy(j).wait_send()
        return carry

    lax.fori_loop(1, PLANE, sent, 0)


def on_device(queries, keys, values, truth, widths, node_order):
    bf16 = jnp.bfloat16
    shape = queries.shape
    dma = pltpu.SemaphoreType.DMA
    vmem = pltpu.VMEM
    return pl.pallas_call(
        kernel,
        out_shape=[jax.ShapeDtypeStruct(shape, bf16)] * 3,
        in_specs=[
            pl.BlockSpec(memory_space=pltpu.SMEM),
            pl.BlockSpec(memory_space=pltpu.VMEM),
        ]
        + [pl.BlockSpec(memory_space=pl.ANY)] * 4,
        out_specs=[pl.BlockSpec(memory_space=pltpu.VMEM)] * 3,
        scratch_shapes=[
            vmem((256, 1024), bf16),
            vmem((256, 1024), bf16),
            vmem((256, 1024), bf16),
            vmem((128, 1024), bf16),
            vmem((PLANE, 3 * HEAD, CHUNK), bf16),
            vmem((PLANE + 2, 3 * HEAD, CHUNK), bf16),
            vmem((PLANE, HEAD, BLOCK), bf16),
            vmem((4, HEAD, BLOCK), bf16),
            vmem((PLANE, 3, CHUNK, CHUNK), bf16),
            vmem((UNITS, MEM, HEAD, BLOCK), bf16),
            vmem((UNITS, MEM, HEAD, BLOCK), bf16),
            vmem((UNITS, MEM, HEAD, BLOCK), bf16),
            vmem((UNITS, MEM, HEAD, BLOCK), bf16),
            vmem((PLANE + 2, 2 * HEAD, CHUNK), jnp.float32),
            vmem((2 * HEAD, CHUNK), bf16),
            vmem((2 * HEAD, CHUNK), bf16),
            vmem((PLANE, HEAD, CHUNK), bf16),
            vmem((PLANE + 2, 2 * HEAD, CHUNK), bf16),
            vmem((PLANE, HEAD, CHUNK), bf16),
            vmem((PLANE, 2 * HEAD, CHUNK), bf16),
            dma((4,)),
            dma((16,)),
            dma((16,)),
            dma((16,)),
            dma((4,)),
            dma((2,)),
            dma((2,)),
            dma((UNITS, MEM)),
            dma((UNITS, MEM)),
            dma((UNITS, MEM)),
            dma((UNITS, MEM)),
            dma((2,)),
            dma((2,)),
            dma((PLANE,)),
            dma((PLANE,)),
            dma((PLANE,)),
            dma((PLANE,)),
        ],
        compiler_params=pltpu.CompilerParams(
            collective_id=0, has_side_effects=True, vmem_limit_bytes=48 << 20
        ),
        name="band_attention",
    )(widths, node_order.reshape(1, BLOCK), queries, keys, values, truth)


def solution(mesh):
    placed = (
        P("mem", "grid", None),
        P("mem", "grid", None),
        P("mem", "grid", None),
        P("grid", None),
        P(),
        P(),
    )
    return jax.shard_map(
        on_device,
        mesh=mesh,
        in_specs=placed,
        out_specs=(P("mem", "grid", None), P("mem", "grid", None), P("mem", "grid", None)),
        check_vma=False,
    )
```

```python
import functools

import jax
import jax.numpy as jnp
from jax import lax
from jax.experimental import pallas as pl
from jax.experimental.pallas import tpu as pltpu
from jax.sharding import PartitionSpec as P

HEAD = 64
BLOCK = 128
CHUNK = 2 * BLOCK
PLANE = 16
MEM = 8
UNITS = 4
NEG = -1e30
SMOOTH2 = 0.0625
SHARE = 16
MESH = pl.DeviceIdType.MESH

TN = (((0,), (0,)), ((), ()))
NT = (((1,), (1,)), ((), ()))
NN = (((1,), (0,)), ((), ()))


def dot(a, b, dims):
    return lax.dot_general(a, b, dims, preferred_element_type=jnp.float32)


def slope(diff):
    return diff * lax.rsqrt(diff * diff + SMOOTH2)


def kernel(
    widths, order, q_hbm, k_hbm, v_hbm, t_hbm,
    dq_out, dk_out, dv_out,
    q_in, k_in, v_in, t_in,
    stage, ext, k_nat, v_nat, tstage, tgt, weights, share, out_u, ens, gout, g_u, acc, back_low, back_high,
    dq_src, dkv_src, dq_dst, dkv_dst,
    load_sem, in_send, in_recv, t_send, t_recv, halo_send, halo_recv,
    m1_send, m1_recv, m2_send, m2_recv, back_send, back_recv,
    dq_send, dq_recv, dkv_send, dkv_recv,
):
    grid = lax.axis_index("grid")
    mem = lax.axis_index("mem")
    z_hi = grid // 16
    x = (grid // 4) % 4
    y = grid % 4
    p = grid % 16
    z_lo = mem // 2
    core = mem % 2
    f32, bf16 = jnp.float32, jnp.bfloat16

    def at_plane(xx, yy):
        return (z_hi * 16 + (xx % 4) * 4 + yy % 4, mem)

    def at_z(d):
        return (((z_hi + d) % 4) * 16 + p, mem)

    own_rows = pl.ds(pl.multiple_of(z_lo * SHARE, SHARE), SHARE)
    loads = [
        pltpu.make_async_copy(src.at[0], dst, load_sem.at[i])
        for i, (src, dst) in enumerate(((q_hbm, q_in), (k_hbm, k_in), (v_hbm, v_in)))
    ]
    for load in loads:
        load.start()
    load_truth = pltpu.make_async_copy(
        t_hbm.at[pl.ds(pl.multiple_of(core * BLOCK, BLOCK), BLOCK)], t_in, load_sem.at[3]
    )
    load_truth.start()

    offsets = [(dx, dy) for dx in (0, 3, 2, 1) for dy in (1, 3, 2, 0)]
    offsets.remove((0, 0))
    barrier = pltpu.get_barrier_semaphore()
    for dx, dy in offsets:
        pl.semaphore_signal(barrier, inc=1, device_id=at_plane(x + dx, y + dy), device_id_type=MESH)
    for o in range(1, MEM):
        pl.semaphore_signal(barrier, inc=1, device_id=(grid, (mem + o) % MEM), device_id_type=MESH)
    for d in (1, 3):
        pl.semaphore_signal(barrier, inc=1, device_id=at_z(d), device_id_type=MESH)

    for load in loads:
        load.wait()

    def to_stage(pair, parts):
        lanes = pl.ds(pl.multiple_of(pair * 128, 128), 128)
        for i in parts:
            block = (q_in, k_in, v_in)[i][:, lanes]
            if i == 0:
                block = block * bf16(0.125)
            block = block.T
            stage[pair * 2, pl.ds(i * HEAD, HEAD)] = block[:HEAD]
            stage[pair * 2 + 1, pl.ds(i * HEAD, HEAD)] = block[HEAD:]

    part_rows = (pl.ds(0, 2 * HEAD), pl.ds(2 * HEAD, HEAD))

    def in_copy(dx, dy, part):
        target = ((x + dx) % 4) * 4 + (y + dy) % 4
        return pltpu.make_async_remote_copy(
            src_ref=stage.at[target, part_rows[part]],
            dst_ref=ext.at[1 + p, part_rows[part]],
            send_sem=in_send.at[part, dx * 4 + dy],
            recv_sem=in_recv.at[part, dx * 4 + dy],
            device_id=at_plane(x + dx, y + dy),
            device_id_type=MESH,
        )

    for dx in (0, 3, 2, 1):
        row = (x + dx) % 4
        to_stage(row * 2, (0, 1))
        to_stage(row * 2 + 1, (0, 1))
        if dx == 0:
            pl.semaphore_wait(barrier, 15 + 7 + 2)
        for a, b in offsets:
            if a == dx:
                in_copy(a, b, 0).start()

    for pair in range(8):
        to_stage(pair, (2,))
    ext[1 + p] = stage[p]

    load_truth.wait()

    def t_copy(dx, dy):
        return pltpu.make_async_remote_copy(
            src_ref=tstage.at[((x + dx) % 4) * 4 + (y + dy) % 4, own_rows],
            dst_ref=tgt.at[p],
            send_sem=t_send.at[dx * 4 + dy],
            recv_sem=t_recv.at[p],
            device_id=at_plane(x + dx, y + dy),
            device_id_type=MESH,
        )

    nodes = lax.broadcasted_iota(jnp.int32, (BLOCK, BLOCK), 0)
    pick = jnp.where(nodes == order[...], 1.0, 0.0).astype(bf16)
    for pair in range(8):
        ordered = dot(t_in[:, pair * 128 : pair * 128 + 128], pick, TN).astype(bf16)
        tstage[pair * 2] = ordered[:HEAD]
        tstage[pair * 2 + 1] = ordered[HEAD:]
    tgt[p] = tstage[p, own_rows]

    acc[...] = jnp.zeros_like(acc)
    for corner in ((pl.ds(0, BLOCK), pl.ds(BLOCK, BLOCK)), (pl.ds(5 * BLOCK, BLOCK), pl.ds(0, BLOCK))):
        for j in range(PLANE):
            weights[j, corner[0], corner[1]] = jnp.zeros((BLOCK, BLOCK), bf16)

    for dx, dy in offsets:
        in_copy(dx, dy, 0).wait_send()
    for dx, dy in offsets:
        in_copy(dx, dy, 1).start()
    for dx, dy in offsets:
        t_copy(dx, dy).start()

    far = jnp.where(widths[p] >= 2, 0.0, NEG).astype(f32)

    def halo_copy(up, part):
        src, dst = (PLANE, 0) if up else (1, PLANE + 1)
        i = (0 if up else 1) + 2 * part
        rows = pl.ds((1 + part) * HEAD, HEAD)
        return pltpu.make_async_remote_copy(
            src_ref=ext.at[src, rows],
            dst_ref=ext.at[dst, rows],
            send_sem=halo_send.at[i],
            recv_sem=halo_recv.at[i],
            device_id=at_z(1 if up else 3),
            device_id_type=MESH,
        )

    def natural(slot, part):
        (k_nat, v_nat)[part][slot] = ext[slot, pl.ds((1 + part) * HEAD, HEAD)].T

    def all_natural(part):
        def one(slot, carry):
            natural(slot, part)
            return carry

        lax.fori_loop(1, PLANE + 1, one, 0)

    def arrive(part):
        for dx, dy in offsets:
            in_copy(dx, dy, part).wait_recv()
        for up in (True, False):
            halo_copy(up, part).start()

    def arrive_halos(part):
        for up in (True, False):
            halo_copy(up, part).wait_recv()
        natural(0, part)
        natural(PLANE + 1, part)

    def unit_of(k):
        unit = (x + 1 + k) % 4
        return jnp.where(x == 2, 3 * k, unit) if k < 2 else unit

    def m1_copy(k, o):
        to = (mem + o) % MEM
        return pltpu.make_async_remote_copy(
            src_ref=out_u.at[k, to % 2, pl.ds(pl.multiple_of(to // 2 * SHARE, SHARE), SHARE)],
            dst_ref=ens.at[k, mem],
            send_sem=m1_send.at[k, o],
            recv_sem=m1_recv.at[k, o],
            device_id=(grid, (mem + o) % MEM),
            device_id_type=MESH,
        )

    def m2_copy(k, o):
        return pltpu.make_async_remote_copy(
            src_ref=gout.at[k, (mem + o) % MEM],
            dst_ref=g_u.at[k, core, own_rows],
            send_sem=m2_send.at[k, o],
            recv_sem=m2_recv.at[k, o],
            device_id=(grid, (mem + o) % MEM),
            device_id_type=MESH,
        )

    def lanes_of(i):
        return pl.ds(pl.multiple_of(i * BLOCK, BLOCK), BLOCK)

    def chunk_of(k, i):
        return (unit_of(k) * 4 + 1 + i) % PLANE

    def score(unit):
        def one(i, carry):
            j = (unit * 4 + 1 + i) % PLANE
            q_t = ext[j + 1, pl.ds(0, HEAD)]
            scores = [dot(k_nat[j + t], q_t, NN) for t in range(3)]
            for h in range(2):
                lanes = slice(h * BLOCK, h * BLOCK + BLOCK)
                tiles = []
                for n in range(5):
                    top = (h + n) % 2 * BLOCK
                    tiles.append(scores[(h + n) // 2][top : top + BLOCK, lanes])
                tiles[0] = tiles[0] + far
                tiles[4] = tiles[4] + far
                highest = functools.reduce(jnp.maximum, tiles)
                highest = jnp.max(highest, axis=0, keepdims=True)
                total = jnp.zeros((BLOCK, BLOCK), f32)
                for n in range(5):
                    term = jnp.exp(tiles[n] - highest)
                    total = total + term
                    weights[j, pl.ds((h + n) * BLOCK, BLOCK), lanes] = term.astype(bf16)
                share[j, :, lanes] = 1.0 / jnp.sum(total, axis=0, keepdims=True)
            return carry

        lax.fori_loop(0, 4, one, 0)

    def mix(k):
        if k == 1:
            arrive_halos(1)
        def one(i, carry):
            j = chunk_of(k, i)
            mixed = jnp.zeros((HEAD, CHUNK), f32)
            for t in range(3):
                mixed = mixed + dot(
                    ext[j + t, pl.ds(2 * HEAD, HEAD)], weights[j, pl.ds(t * CHUNK, CHUNK)], NN
                )
            mixed = (mixed * share[j]).astype(bf16)
            out_u[k, 0, :, lanes_of(i)] = mixed[:, :BLOCK]
            out_u[k, 1, :, lanes_of(i)] = mixed[:, BLOCK:]
            return carry

        lax.fori_loop(0, 4, one, 0)
        ens[k, mem] = out_u[k, core, own_rows]

    def m1_start(k):
        if k > 0:
            for o in range(1, MEM):
                m1_copy(k - 1, o).wait_send()
        for o in (1, 7, 2, 6, 3, 5, 4):
            m1_copy(k, o).start()

    def truth_arrive(k):
        for i in range(4):
            j = chunk_of(k, i)

            @pl.when(j != p)
            def _():
                pltpu.make_async_remote_copy(
                    src_ref=tstage.at[0, own_rows],
                    dst_ref=tgt.at[j],
                    send_sem=t_send.at[0],
                    recv_sem=t_recv.at[j],
                    device_id=(z_hi * 16 + j, mem),
                    device_id_type=MESH,
                ).wait_recv()

    def crps(k):
        truth_arrive(k)
        for o in range(1, MEM):
            m1_copy(k, o).wait_recv()
        own = [ens[k, n].astype(f32) for n in range(MEM)]
        target = jnp.concatenate([tgt[chunk_of(k, i)] for i in range(4)], axis=1).astype(f32)
        totals = [jnp.zeros((SHARE, UNITS * BLOCK), f32) for _ in range(MEM)]
        for a in range(MEM):
            for b in range(a + 1, MEM):
                s = slope(own[a] - own[b])
                totals[a] = totals[a] + s
                totals[b] = totals[b] - s
        for n in range(MEM):
            gout[k, n] = (slope(own[n] - target) - totals[n] * (1.0 / (MEM - 1))).astype(bf16)
        for o in (1, 7, 2, 6, 3, 5, 4):
            m2_copy(k, o).start()
        g_u[k, core, own_rows] = gout[k, mem]

    def dq_copy(j):
        return pltpu.make_async_remote_copy(
            src_ref=dq_src.at[j],
            dst_ref=dq_dst.at[p],
            send_sem=dq_send.at[j],
            recv_sem=dq_recv.at[p],
            device_id=(z_hi * 16 + j, mem),
            device_id_type=MESH,
        )

    def dkv_copy(j):
        return pltpu.make_async_remote_copy(
            src_ref=dkv_src.at[j],
            dst_ref=dkv_dst.at[p],
            send_sem=dkv_send.at[j],
            recv_sem=dkv_recv.at[p],
            device_id=(z_hi * 16 + j, mem),
            device_id_type=MESH,
        )

    def back_copy(down):
        i = 0 if down else 1
        return pltpu.make_async_remote_copy(
            src_ref=dkv_src.at[PLANE + i],
            dst_ref=(back_high if down else back_low),
            send_sem=back_send.at[i],
            recv_sem=back_recv.at[i],
            device_id=at_z(3 if down else 1),
            device_id_type=MESH,
        )

    def finish_dkv(j):
        dkv_src[j] = acc[j + 1].astype(bf16)

        @pl.when(j != p)
        def _():
            dkv_copy(j).start()

        @pl.when(j == p)
        def _():
            dkv_dst[p] = dkv_src[p]

    def finish_ends():
        back_copy(True).wait_recv()
        acc[PLANE] += back_high[...].astype(f32)
        finish_dkv(PLANE - 1)
        back_copy(False).wait_recv()
        acc[1] += back_low[...].astype(f32)
        finish_dkv(0)

    left = lax.broadcasted_iota(jnp.int32, (CHUNK, 2 * HEAD), 1) < HEAD

    def backward(k):
        for o in range(1, MEM):
            m2_copy(k, o).wait_recv()

        def one(i):
            j = chunk_of(k, i)
            g_t = jnp.concatenate([g_u[k, c, :, lanes_of(i)] for c in range(2)], axis=1).astype(f32)
            o_t = jnp.concatenate([out_u[k, c, :, lanes_of(i)] for c in range(2)], axis=1).astype(f32)
            scale = share[j]
            inner = jnp.sum(g_t * o_t, axis=0, keepdims=True) * scale
            g_t = (g_t * scale).astype(bf16)
            both = jnp.concatenate([ext[j + 1, pl.ds(0, HEAD)], g_t], axis=0).T
            q_side = jnp.where(left, both, bf16(0))
            g_side = jnp.where(left, bf16(0), both)
            dq = jnp.zeros((HEAD, CHUNK), f32)
            for t in range(3):
                along = dot(v_nat[j + t], g_t, NN)
                low = weights[j, pl.ds(t * CHUNK, CHUNK)]
                ds = (low.astype(f32) * (along - inner)).astype(bf16)
                dq = dq + dot(ext[j + t, pl.ds(HEAD, HEAD)], ds, NN)
                acc[j + t] += dot(ds, q_side, NN) + dot(low, g_side, NN)
            dq_src[j] = (dq * 0.125).astype(bf16)

            @pl.when(j != p)
            def _():
                dq_copy(j).start()

            @pl.when(j == p)
            def _():
                dq_dst[p] = dq_src[p]

        def ends(n, carry):
            one(3 - n)
            return carry

        lax.fori_loop(0, 2, ends, 0)

        @pl.when(unit_of(k) == 3)
        def _():
            dkv_src[PLANE] = acc[0].astype(bf16)
            back_copy(True).start()
            dkv_src[PLANE + 1] = acc[PLANE + 1].astype(bf16)
            back_copy(False).start()

        def others(i, carry):
            one(i)
            return carry

        lax.fori_loop(0, 2, others, 0)

        def done(i, carry):
            j = (unit_of(k) * 4 + i) % PLANE

            @pl.when((j != 0) & (j != PLANE - 1))
            def _():
                finish_dkv(j)

            return carry

        if k == 1:

            @pl.when(x == 2)
            def _():
                finish_dkv(PLANE - 2)
                finish_dkv(1)

            @pl.when(x != 2)
            def _():
                lax.fori_loop(0, 4, done, 0)
        else:
            lax.fori_loop(2 if k == 0 else 0, 6 if k == UNITS - 1 else 4, done, 0)
        if k == 2:
            pl.when((x == 1) | (x == 2))(finish_ends)
        if k == 3:
            pl.when((x == 0) | (x == 3))(finish_ends)

    arrive(0)
    all_natural(0)
    for unit in range(3):
        score(unit)
    arrive(1)
    mix(0)
    m1_start(0)
    arrive_halos(0)
    score(3)
    mix(1)
    mix(2)
    mix(3)
    m1_start(1)
    all_natural(1)
    crps(0)
    m1_start(2)
    crps(1)
    m1_start(3)
    backward(0)
    crps(2)
    backward(1)
    crps(3)
    backward(2)
    backward(3)

    def all_arrived(ref, recv):
        def one(n, carry):
            src = (p + n) % PLANE
            pltpu.make_async_remote_copy(
                src_ref=ref.at[src], dst_ref=ref.at[src], send_sem=dq_send.at[0], recv_sem=recv.at[src],
                device_id=(z_hi * 16 + src, mem), device_id_type=MESH,
            ).wait_recv()
            return carry

        lax.fori_loop(1, PLANE, one, 0)

    all_arrived(dq_dst, dq_recv)
    for pair in range(8):
        block = jnp.concatenate([dq_dst[2 * pair], dq_dst[2 * pair + 1]], axis=0)
        dq_out[0, :, pair * 128 : pair * 128 + 128] = block.T
    all_arrived(dkv_dst, dkv_recv)
    for pair in range(8):
        even, odd = dkv_dst[2 * pair], dkv_dst[2 * pair + 1]
        lanes = slice(pair * 128, pair * 128 + 128)
        dk_out[0, :, lanes] = jnp.concatenate([even[:, :HEAD], odd[:, :HEAD]], axis=1)
        dv_out[0, :, lanes] = jnp.concatenate([even[:, HEAD:], odd[:, HEAD:]], axis=1)

    for dx, dy in offsets:
        in_copy(dx, dy, 1).wait_send()
    for up in (True, False):
        for part in range(2):
            halo_copy(up, part).wait_send()
        back_copy(up).wait_send()
    for o in range(1, MEM):
        m1_copy(UNITS - 1, o).wait_send()
        for k in range(UNITS):
            m2_copy(k, o).wait_send()

    for dx, dy in offsets:
        t_copy(dx, dy).wait_send()

    def sent(n, carry):
        j = (p + n) % PLANE
        dq_copy(j).wait_send()
        dkv_copy(j).wait_send()
        return carry

    lax.fori_loop(1, PLANE, sent, 0)


def on_device(queries, keys, values, truth, widths, node_order):
    bf16 = jnp.bfloat16
    shape = queries.shape
    dma = pltpu.SemaphoreType.DMA
    vmem = pltpu.VMEM
    return pl.pallas_call(
        kernel,
        out_shape=[jax.ShapeDtypeStruct(shape, bf16)] * 3,
        in_specs=[
            pl.BlockSpec(memory_space=pltpu.SMEM),
            pl.BlockSpec(memory_space=pltpu.VMEM),
        ]
        + [pl.BlockSpec(memory_space=pl.ANY)] * 4,
        out_specs=[pl.BlockSpec(memory_space=pltpu.VMEM)] * 3,
        scratch_shapes=[
            vmem((256, 1024), bf16),
            vmem((256, 1024), bf16),
            vmem((256, 1024), bf16),
            vmem((128, 1024), bf16),
            vmem((PLANE, 3 * HEAD, CHUNK), bf16),
            vmem((PLANE + 2, 3 * HEAD, CHUNK), bf16),
            vmem((PLANE + 2, CHUNK, HEAD), bf16),
            vmem((PLANE + 2, CHUNK, HEAD), bf16),
            vmem((PLANE, HEAD, BLOCK), bf16),
            vmem((PLANE, SHARE, BLOCK), bf16),
            vmem((PLANE, 3 * CHUNK, CHUNK), bf16),
            vmem((PLANE, 1, CHUNK), jnp.float32),
            vmem((UNITS, 2, HEAD, 4 * BLOCK), bf16),
            vmem((UNITS, MEM, SHARE, 4 * BLOCK), bf16),
            vmem((UNITS, MEM, SHARE, 4 * BLOCK), bf16),
            vmem((UNITS, 2, HEAD, 4 * BLOCK), bf16),
            vmem((PLANE + 2, CHUNK, 2 * HEAD), jnp.float32),
            vmem((CHUNK, 2 * HEAD), bf16),
            vmem((CHUNK, 2 * HEAD), bf16),
            vmem((PLANE, HEAD, CHUNK), bf16),
            vmem((PLANE + 2, CHUNK, 2 * HEAD), bf16),
            vmem((PLANE, HEAD, CHUNK), bf16),
            vmem((PLANE, CHUNK, 2 * HEAD), bf16),
            dma((4,)),
            dma((2, 16)),
            dma((2, 16)),
            dma((16,)),
            dma((16,)),
            dma((4,)),
            dma((4,)),
            dma((UNITS, MEM)),
            dma((UNITS, MEM)),
            dma((UNITS, MEM)),
            dma((UNITS, MEM)),
            dma((2,)),
            dma((2,)),
            dma((PLANE,)),
            dma((PLANE,)),
            dma((PLANE,)),
            dma((PLANE,)),
        ],
        compiler_params=pltpu.CompilerParams(
            collective_id=0, has_side_effects=True, vmem_limit_bytes=62 << 20
        ),
        name="band_attention",
    )(widths, node_order.reshape(1, BLOCK), queries, keys, values, truth)


def solution(mesh):
    placed = (
        P("mem", "grid", None),
        P("mem", "grid", None),
        P("mem", "grid", None),
        P("grid", None),
        P(),
        P(),
    )
    return jax.shard_map(
        on_device,
        mesh=mesh,
        in_specs=placed,
        out_specs=(P("mem", "grid", None), P("mem", "grid", None), P("mem", "grid", None)),
        check_vma=False,
    )
```

```python
import functools

import jax
import jax.numpy as jnp
from jax import lax
from jax.experimental import pallas as pl
from jax.experimental.pallas import tpu as pltpu
from jax.sharding import PartitionSpec as P

HEAD = 64
BLOCK = 128
CHUNK = 2 * BLOCK
PLANE = 16
MEM = 8
UNITS = 4
NEG = -1e30
SMOOTH2 = 0.0625
SHARE = 16
MESH = pl.DeviceIdType.MESH

TN = (((0,), (0,)), ((), ()))
NT = (((1,), (1,)), ((), ()))
NN = (((1,), (0,)), ((), ()))


def dot(a, b, dims):
    return lax.dot_general(a, b, dims, preferred_element_type=jnp.float32)


def slope(diff):
    return diff * lax.rsqrt(diff * diff + SMOOTH2)


def kernel(
    widths, order, q_hbm, k_hbm, v_hbm, t_hbm,
    dq_dst, dkv_dst,
    q_in, k_in, v_in, t_in,
    stage, ext, k_nat, v_nat, tstage, tgt, weights, share, out_u, ens, gout, g_u, acc, back_low, back_high,
    dq_src, dkv_src,
    load_sem, in_send, in_recv, t_send, t_recv, halo_send, halo_recv,
    m1_send, m1_recv, m2_send, m2_recv, back_send, back_recv,
    dq_send, dq_recv, dkv_send, dkv_recv,
):
    grid = lax.axis_index("grid")
    mem = lax.axis_index("mem")
    z_hi = grid // 16
    x = (grid // 4) % 4
    y = grid % 4
    p = grid % 16
    z_lo = mem // 2
    core = mem % 2
    f32, bf16 = jnp.float32, jnp.bfloat16

    def at_plane(xx, yy):
        return (z_hi * 16 + (xx % 4) * 4 + yy % 4, mem)

    def at_z(d):
        return (((z_hi + d) % 4) * 16 + p, mem)

    own_rows = pl.ds(pl.multiple_of(z_lo * SHARE, SHARE), SHARE)
    loads = [
        pltpu.make_async_copy(src.at[0], dst, load_sem.at[i])
        for i, (src, dst) in enumerate(((q_hbm, q_in), (k_hbm, k_in), (v_hbm, v_in)))
    ]
    for load in loads:
        load.start()
    load_truth = pltpu.make_async_copy(
        t_hbm.at[pl.ds(pl.multiple_of(core * BLOCK, BLOCK), BLOCK)], t_in, load_sem.at[3]
    )
    load_truth.start()

    offsets = [(dx, dy) for dx in (0, 3, 2, 1) for dy in (1, 3, 2, 0)]
    offsets.remove((0, 0))
    barrier = pltpu.get_barrier_semaphore()
    for dx, dy in offsets:
        pl.semaphore_signal(barrier, inc=1, device_id=at_plane(x + dx, y + dy), device_id_type=MESH)
    for o in range(1, MEM):
        pl.semaphore_signal(barrier, inc=1, device_id=(grid, (mem + o) % MEM), device_id_type=MESH)
    for d in (1, 3):
        pl.semaphore_signal(barrier, inc=1, device_id=at_z(d), device_id_type=MESH)

    for load in loads:
        load.wait()

    def to_stage(pair, parts):
        lanes = pl.ds(pl.multiple_of(pair * 128, 128), 128)
        for i in parts:
            block = (q_in, k_in, v_in)[i][:, lanes]
            if i == 0:
                block = block * bf16(0.125)
            block = block.T
            stage[pair * 2, pl.ds(i * HEAD, HEAD)] = block[:HEAD]
            stage[pair * 2 + 1, pl.ds(i * HEAD, HEAD)] = block[HEAD:]

    is_end = (p == 0) | (p == PLANE - 1)
    part_rows = (
        pl.ds(pl.multiple_of(jnp.where(is_end, HEAD, 0), HEAD), 2 * HEAD),
        pl.ds(pl.multiple_of(jnp.where(is_end, 0, 2 * HEAD), HEAD), HEAD),
    )

    def in_copy(dx, dy, part):
        target = ((x + dx) % 4) * 4 + (y + dy) % 4
        return pltpu.make_async_remote_copy(
            src_ref=stage.at[target, part_rows[part]],
            dst_ref=ext.at[1 + p, part_rows[part]],
            send_sem=in_send.at[part, dx * 4 + dy],
            recv_sem=in_recv.at[part, dx * 4 + dy],
            device_id=at_plane(x + dx, y + dy),
            device_id_type=MESH,
        )

    for dx in (0, 3, 2, 1):
        row = (x + dx) % 4
        to_stage(row * 2, (0, 1, 2))
        to_stage(row * 2 + 1, (0, 1, 2))
        if dx == 0:
            pl.semaphore_wait(barrier, 15 + 7 + 2)
        for a, b in offsets:
            if a == dx:
                in_copy(a, b, 0).start()

    ext[1 + p] = stage[p]

    load_truth.wait()

    def t_copy(dx, dy):
        return pltpu.make_async_remote_copy(
            src_ref=tstage.at[((x + dx) % 4) * 4 + (y + dy) % 4, own_rows],
            dst_ref=tgt.at[p],
            send_sem=t_send.at[dx * 4 + dy],
            recv_sem=t_recv.at[p],
            device_id=at_plane(x + dx, y + dy),
            device_id_type=MESH,
        )

    nodes = lax.broadcasted_iota(jnp.int32, (BLOCK, BLOCK), 0)
    pick = jnp.where(nodes == order[...], 1.0, 0.0).astype(bf16)
    for pair in range(8):
        ordered = dot(t_in[:, pair * 128 : pair * 128 + 128], pick, TN).astype(bf16)
        tstage[pair * 2] = ordered[:HEAD]
        tstage[pair * 2 + 1] = ordered[HEAD:]
    tgt[p] = tstage[p, own_rows]

    acc[...] = jnp.zeros_like(acc)
    for corner in ((pl.ds(0, BLOCK), pl.ds(BLOCK, BLOCK)), (pl.ds(5 * BLOCK, BLOCK), pl.ds(0, BLOCK))):
        for j in range(PLANE):
            weights[j, corner[0], corner[1]] = jnp.zeros((BLOCK, BLOCK), bf16)

    for dx, dy in offsets:
        in_copy(dx, dy, 0).wait_send()
    for dx, dy in offsets:
        in_copy(dx, dy, 1).start()
    for dx, dy in offsets:
        t_copy(dx, dy).start()

    far = jnp.where(widths[p] >= 2, 0.0, NEG).astype(f32)

    def halo_copy(up, part):
        src, dst = (PLANE, 0) if up else (1, PLANE + 1)
        i = (0 if up else 1) + 2 * part
        rows = pl.ds((1 + part) * HEAD, HEAD)
        return pltpu.make_async_remote_copy(
            src_ref=ext.at[src, rows],
            dst_ref=ext.at[dst, rows],
            send_sem=halo_send.at[i],
            recv_sem=halo_recv.at[i],
            device_id=at_z(1 if up else 3),
            device_id_type=MESH,
        )

    def natural(slot, part):
        (k_nat, v_nat)[part][slot] = ext[slot, pl.ds((1 + part) * HEAD, HEAD)].T

    def all_natural(part):
        def one(slot, carry):
            natural(slot, part)
            return carry

        lax.fori_loop(1, PLANE + 1, one, 0)

    def arrive(part):
        for dx, dy in offsets:
            in_copy(dx, dy, part).wait_recv()
        if part == 0:
            for up in (True, False):
                halo_copy(up, 0).start()
                halo_copy(up, 1).start()

    def arrive_halos(part):
        for up in (True, False):
            halo_copy(up, part).wait_recv()
        natural(0, part)
        natural(PLANE + 1, part)

    def unit_of(k):
        unit = (x + 1 + k) % 4
        return jnp.where(x == 2, 3 * k, unit) if k < 2 else unit

    def m1_copy(k, o):
        to = (mem + o) % MEM
        return pltpu.make_async_remote_copy(
            src_ref=out_u.at[k, to % 2, pl.ds(pl.multiple_of(to // 2 * SHARE, SHARE), SHARE)],
            dst_ref=ens.at[k, mem],
            send_sem=m1_send.at[k, o],
            recv_sem=m1_recv.at[k, o],
            device_id=(grid, (mem + o) % MEM),
            device_id_type=MESH,
        )

    def m2_copy(k, o):
        return pltpu.make_async_remote_copy(
            src_ref=gout.at[k, (mem + o) % MEM],
            dst_ref=g_u.at[k, core, own_rows],
            send_sem=m2_send.at[k, o],
            recv_sem=m2_recv.at[k, o],
            device_id=(grid, (mem + o) % MEM),
            device_id_type=MESH,
        )

    def lanes_of(i):
        return pl.ds(pl.multiple_of(i * BLOCK, BLOCK), BLOCK)

    def chunk_of(k, i):
        return (unit_of(k) * 4 + 1 + i) % PLANE

    def score(unit):
        def one(i, carry):
            j = (unit * 4 + 1 + i) % PLANE
            q_t = ext[j + 1, pl.ds(0, HEAD)]
            scores = [dot(k_nat[j + t], q_t, NN) for t in range(3)]
            for h in range(2):
                lanes = slice(h * BLOCK, h * BLOCK + BLOCK)
                tiles = []
                for n in range(5):
                    top = (h + n) % 2 * BLOCK
                    tiles.append(scores[(h + n) // 2][top : top + BLOCK, lanes])
                tiles[0] = tiles[0] + far
                tiles[4] = tiles[4] + far
                highest = functools.reduce(jnp.maximum, tiles)
                highest = jnp.max(highest, axis=0, keepdims=True)
                total = jnp.zeros((BLOCK, BLOCK), f32)
                for n in range(5):
                    term = jnp.exp(tiles[n] - highest)
                    total = total + term
                    weights[j, pl.ds((h + n) * BLOCK, BLOCK), lanes] = term.astype(bf16)
                share[j, :, lanes] = 1.0 / jnp.sum(total, axis=0, keepdims=True)
            return carry

        lax.fori_loop(0, 4, one, 0)

    def mix(k):
        if k == 1:
            arrive_halos(1)
        def one(i, carry):
            j = chunk_of(k, i)
            mixed = jnp.zeros((HEAD, CHUNK), f32)
            for t in range(3):
                mixed = mixed + dot(
                    ext[j + t, pl.ds(2 * HEAD, HEAD)], weights[j, pl.ds(t * CHUNK, CHUNK)], NN
                )
            mixed = (mixed * share[j]).astype(bf16)
            out_u[k, 0, :, lanes_of(i)] = mixed[:, :BLOCK]
            out_u[k, 1, :, lanes_of(i)] = mixed[:, BLOCK:]
            return carry

        lax.fori_loop(0, 4, one, 0)
        ens[k, mem] = out_u[k, core, own_rows]

    def m1_start(k):
        if k > 0:
            for o in range(1, MEM):
                m1_copy(k - 1, o).wait_send()
        for o in (1, 7, 2, 6, 3, 5, 4):
            m1_copy(k, o).start()

    def truth_arrive(k):
        for i in range(4):
            j = chunk_of(k, i)

            @pl.when(j != p)
            def _():
                pltpu.make_async_remote_copy(
                    src_ref=tstage.at[0, own_rows],
                    dst_ref=tgt.at[j],
                    send_sem=t_send.at[0],
                    recv_sem=t_recv.at[j],
                    device_id=(z_hi * 16 + j, mem),
                    device_id_type=MESH,
                ).wait_recv()

    def crps(k):
        truth_arrive(k)
        for o in range(1, MEM):
            m1_copy(k, o).wait_recv()
        own = [ens[k, n].astype(f32) for n in range(MEM)]
        target = jnp.concatenate([tgt[chunk_of(k, i)] for i in range(4)], axis=1).astype(f32)
        totals = [jnp.zeros((SHARE, UNITS * BLOCK), f32) for _ in range(MEM)]
        for a in range(MEM):
            for b in range(a + 1, MEM):
                s = slope(own[a] - own[b])
                totals[a] = totals[a] + s
                totals[b] = totals[b] - s
        for n in range(MEM):
            gout[k, n] = (slope(own[n] - target) - totals[n] * (1.0 / (MEM - 1))).astype(bf16)
        for o in (1, 7, 2, 6, 3, 5, 4):
            m2_copy(k, o).start()
        g_u[k, core, own_rows] = gout[k, mem]

    def dq_copy(j):
        return pltpu.make_async_remote_copy(
            src_ref=dq_src.at[j],
            dst_ref=dq_dst.at[p],
            send_sem=dq_send.at[j],
            recv_sem=dq_recv.at[p],
            device_id=(z_hi * 16 + j, mem),
            device_id_type=MESH,
        )

    def dkv_copy(j):
        return pltpu.make_async_remote_copy(
            src_ref=dkv_src.at[j],
            dst_ref=dkv_dst.at[p],
            send_sem=dkv_send.at[j],
            recv_sem=dkv_recv.at[p],
            device_id=(z_hi * 16 + j, mem),
            device_id_type=MESH,
        )

    def back_copy(down):
        i = 0 if down else 1
        return pltpu.make_async_remote_copy(
            src_ref=dkv_src.at[PLANE + i],
            dst_ref=(back_high if down else back_low),
            send_sem=back_send.at[i],
            recv_sem=back_recv.at[i],
            device_id=at_z(3 if down else 1),
            device_id_type=MESH,
        )

    def finish_dkv(j):
        dkv_src[j] = acc[j + 1].astype(bf16)

        @pl.when(j != p)
        def _():
            dkv_copy(j).start()

        @pl.when(j == p)
        def _():
            dkv_dst[p] = dkv_src[p]

    def finish_ends():
        back_copy(True).wait_recv()
        acc[PLANE] += back_high[...].astype(f32)
        finish_dkv(PLANE - 1)
        back_copy(False).wait_recv()
        acc[1] += back_low[...].astype(f32)
        finish_dkv(0)

    left = lax.broadcasted_iota(jnp.int32, (CHUNK, 2 * HEAD), 1) < HEAD

    def backward(k):
        for o in range(1, MEM):
            m2_copy(k, o).wait_recv()

        def one(i):
            j = chunk_of(k, i)
            g_t = jnp.concatenate([g_u[k, c, :, lanes_of(i)] for c in range(2)], axis=1).astype(f32)
            o_t = jnp.concatenate([out_u[k, c, :, lanes_of(i)] for c in range(2)], axis=1).astype(f32)
            scale = share[j]
            inner = jnp.sum(g_t * o_t, axis=0, keepdims=True) * scale
            g_t = (g_t * scale).astype(bf16)
            both = jnp.concatenate([ext[j + 1, pl.ds(0, HEAD)], g_t], axis=0).T
            q_side = jnp.where(left, both, bf16(0))
            g_side = jnp.where(left, bf16(0), both)
            dq = jnp.zeros((HEAD, CHUNK), f32)
            for t in range(3):
                along = dot(v_nat[j + t], g_t, NN)
                low = weights[j, pl.ds(t * CHUNK, CHUNK)]
                ds = (low.astype(f32) * (along - inner)).astype(bf16)
                dq = dq + dot(ext[j + t, pl.ds(HEAD, HEAD)], ds, NN)
                acc[j + t] += dot(ds, q_side, NN) + dot(low, g_side, NN)
            dq_src[j] = (dq * 0.125).astype(bf16)

            @pl.when(j != p)
            def _():
                dq_copy(j).start()

            @pl.when(j == p)
            def _():
                dq_dst[p] = dq_src[p]

        def ends(n, carry):
            one(3 - n)
            return carry

        lax.fori_loop(0, 2, ends, 0)

        @pl.when(unit_of(k) == 3)
        def _():
            dkv_src[PLANE] = acc[0].astype(bf16)
            back_copy(True).start()
            dkv_src[PLANE + 1] = acc[PLANE + 1].astype(bf16)
            back_copy(False).start()

        def others(i, carry):
            one(i)
            return carry

        lax.fori_loop(0, 2, others, 0)

        def done(i, carry):
            j = (unit_of(k) * 4 + i) % PLANE

            @pl.when((j != 0) & (j != PLANE - 1))
            def _():
                finish_dkv(j)

            return carry

        if k == 1:

            @pl.when(x == 2)
            def _():
                finish_dkv(PLANE - 2)
                finish_dkv(1)

            @pl.when(x != 2)
            def _():
                lax.fori_loop(0, 4, done, 0)
        else:
            lax.fori_loop(2 if k == 0 else 0, 6 if k == UNITS - 1 else 4, done, 0)
        if k == 2:
            pl.when((x == 1) | (x == 2))(finish_ends)
        if k == 3:
            pl.when((x == 0) | (x == 3))(finish_ends)

    arrive(0)
    all_natural(0)
    for unit in range(3):
        score(unit)
    arrive(1)
    mix(0)
    m1_start(0)
    arrive_halos(0)
    score(3)
    mix(1)
    mix(2)
    mix(3)
    m1_start(1)
    all_natural(1)
    crps(0)
    m1_start(2)
    crps(1)
    m1_start(3)
    backward(0)
    crps(2)
    backward(1)
    crps(3)
    backward(2)
    backward(3)

    def all_arrived(ref, recv):
        def one(n, carry):
            src = (p + n) % PLANE
            pltpu.make_async_remote_copy(
                src_ref=ref.at[src], dst_ref=ref.at[src], send_sem=dq_send.at[0], recv_sem=recv.at[src],
                device_id=(z_hi * 16 + src, mem), device_id_type=MESH,
            ).wait_recv()
            return carry

        lax.fori_loop(1, PLANE, one, 0)

    all_arrived(dq_dst, dq_recv)
    all_arrived(dkv_dst, dkv_recv)
    for dx, dy in offsets:
        in_copy(dx, dy, 1).wait_send()
    for up in (True, False):
        for part in range(2):
            halo_copy(up, part).wait_send()
        back_copy(up).wait_send()
    for o in range(1, MEM):
        m1_copy(UNITS - 1, o).wait_send()
        for k in range(UNITS):
            m2_copy(k, o).wait_send()

    for dx, dy in offsets:
        t_copy(dx, dy).wait_send()

    def sent(n, carry):
        j = (p + n) % PLANE
        dq_copy(j).wait_send()
        dkv_copy(j).wait_send()
        return carry

    lax.fori_loop(1, PLANE, sent, 0)


def assemble(dq, dkv, dq_out, dk_out, dv_out):
    for pair in range(dq.shape[0] // 2):
        lanes = slice(pair * 128, pair * 128 + 128)
        dq_out[0, :, lanes] = jnp.concatenate([dq[2 * pair], dq[2 * pair + 1]], axis=0).T
        even, odd = dkv[2 * pair], dkv[2 * pair + 1]
        dk_out[0, :, lanes] = jnp.concatenate([even[:, :HEAD], odd[:, :HEAD]], axis=1)
        dv_out[0, :, lanes] = jnp.concatenate([even[:, HEAD:], odd[:, HEAD:]], axis=1)


def on_device(queries, keys, values, truth, widths, node_order):
    bf16 = jnp.bfloat16
    shape = queries.shape
    dma = pltpu.SemaphoreType.DMA
    vmem = pltpu.VMEM
    dq, dkv = pl.pallas_call(
        kernel,
        out_shape=[
            jax.ShapeDtypeStruct((PLANE, HEAD, CHUNK), bf16),
            jax.ShapeDtypeStruct((PLANE, CHUNK, 2 * HEAD), bf16),
        ],
        in_specs=[
            pl.BlockSpec(memory_space=pltpu.SMEM),
            pl.BlockSpec(memory_space=pltpu.VMEM),
        ]
        + [pl.BlockSpec(memory_space=pl.ANY)] * 4,
        out_specs=[pl.BlockSpec(memory_space=pltpu.VMEM)] * 2,
        scratch_shapes=[
            vmem((256, 1024), bf16),
            vmem((256, 1024), bf16),
            vmem((256, 1024), bf16),
            vmem((128, 1024), bf16),
            vmem((PLANE, 3 * HEAD, CHUNK), bf16),
            vmem((PLANE + 2, 3 * HEAD, CHUNK), bf16),
            vmem((PLANE + 2, CHUNK, HEAD), bf16),
            vmem((PLANE + 2, CHUNK, HEAD), bf16),
            vmem((PLANE, HEAD, BLOCK), bf16),
            vmem((PLANE, SHARE, BLOCK), bf16),
            vmem((PLANE, 3 * CHUNK, CHUNK), bf16),
            vmem((PLANE, 1, CHUNK), jnp.float32),
            vmem((UNITS, 2, HEAD, 4 * BLOCK), bf16),
            vmem((UNITS, MEM, SHARE, 4 * BLOCK), bf16),
            vmem((UNITS, MEM, SHARE, 4 * BLOCK), bf16),
            vmem((UNITS, 2, HEAD, 4 * BLOCK), bf16),
            vmem((PLANE + 2, CHUNK, 2 * HEAD), jnp.float32),
            vmem((CHUNK, 2 * HEAD), bf16),
            vmem((CHUNK, 2 * HEAD), bf16),
            vmem((PLANE, HEAD, CHUNK), bf16),
            vmem((PLANE + 2, CHUNK, 2 * HEAD), bf16),
            dma((4,)),
            dma((2, 16)),
            dma((2, 16)),
            dma((16,)),
            dma((16,)),
            dma((4,)),
            dma((4,)),
            dma((UNITS, MEM)),
            dma((UNITS, MEM)),
            dma((UNITS, MEM)),
            dma((UNITS, MEM)),
            dma((2,)),
            dma((2,)),
            dma((PLANE,)),
            dma((PLANE,)),
            dma((PLANE,)),
            dma((PLANE,)),
        ],
        compiler_params=pltpu.CompilerParams(
            collective_id=0, has_side_effects=True, vmem_limit_bytes=62 << 20
        ),
        name="band_attention",
    )(widths, node_order.reshape(1, BLOCK), queries, keys, values, truth)
    steps = 4
    heads = PLANE // steps
    return pl.pallas_call(
        assemble,
        grid=(steps,),
        out_shape=[jax.ShapeDtypeStruct(shape, bf16)] * 3,
        in_specs=[
            pl.BlockSpec((heads, HEAD, CHUNK), lambda i: (i, 0, 0)),
            pl.BlockSpec((heads, CHUNK, 2 * HEAD), lambda i: (i, 0, 0)),
        ],
        out_specs=[pl.BlockSpec((1, CHUNK, heads * HEAD), lambda i: (0, 0, i))] * 3,
        name="assemble",
    )(dq, dkv)


def solution(mesh):
    placed = (
        P("mem", "grid", None),
        P("mem", "grid", None),
        P("mem", "grid", None),
        P("grid", None),
        P(),
        P(),
    )
    return jax.shard_map(
        on_device,
        mesh=mesh,
        in_specs=placed,
        out_specs=(P("mem", "grid", None), P("mem", "grid", None), P("mem", "grid", None)),
        check_vma=False,
    )
```

```python
import functools

import jax
import jax.numpy as jnp
from jax import lax
from jax.experimental import pallas as pl
from jax.experimental.pallas import tpu as pltpu
from jax.sharding import PartitionSpec as P

HEAD = 64
BLOCK = 128
CHUNK = 2 * BLOCK
PLANE = 16
MEM = 8
UNITS = 4
NEG = -1e30
SMOOTH2 = 0.0625
SHARE = 16
MESH = pl.DeviceIdType.MESH

TN = (((0,), (0,)), ((), ()))
NT = (((1,), (1,)), ((), ()))
NN = (((1,), (0,)), ((), ()))


def dot(a, b, dims):
    return lax.dot_general(a, b, dims, preferred_element_type=jnp.float32)


def slope(diff):
    return diff * lax.rsqrt(diff * diff + SMOOTH2)


def kernel(
    widths, order, q_hbm, k_hbm, v_hbm, t_hbm,
    dq_dst, dkv_dst,
    q_in, k_in, v_in, t_in,
    stage, ext, k_nat, v_nat, tstage, tgt, weights, share, out_u, ens, gout, g_u, acc, back_low, back_high,
    dq_src, dkv_src,
    load_sem, in_send, in_recv, t_send, t_recv, halo_send, halo_recv,
    m1_send, m1_recv, m2_send, m2_recv, back_send, back_recv,
    dq_send, dq_recv, dkv_send, dkv_recv,
):
    grid = lax.axis_index("grid")
    mem = lax.axis_index("mem")
    z_hi = grid // 16
    x = (grid // 4) % 4
    y = grid % 4
    p = grid % 16
    z_lo = mem // 2
    core = mem % 2
    f32, bf16 = jnp.float32, jnp.bfloat16

    def at_plane(xx, yy):
        return (z_hi * 16 + (xx % 4) * 4 + yy % 4, mem)

    def at_z(d):
        return (((z_hi + d) % 4) * 16 + p, mem)

    own_rows = pl.ds(pl.multiple_of(z_lo * SHARE, SHARE), SHARE)
    loads = [
        pltpu.make_async_copy(src.at[0], dst, load_sem.at[i])
        for i, (src, dst) in enumerate(((q_hbm, q_in), (k_hbm, k_in), (v_hbm, v_in)))
    ]
    for load in loads:
        load.start()
    load_truth = pltpu.make_async_copy(
        t_hbm.at[pl.ds(pl.multiple_of(core * BLOCK, BLOCK), BLOCK)], t_in, load_sem.at[3]
    )
    load_truth.start()

    offsets = [(dx, dy) for dx in (0, 3, 2, 1) for dy in (1, 3, 2, 0)]
    offsets.remove((0, 0))
    barrier = pltpu.get_barrier_semaphore()
    for dx, dy in offsets:
        pl.semaphore_signal(barrier, inc=1, device_id=at_plane(x + dx, y + dy), device_id_type=MESH)
    for o in range(1, MEM):
        pl.semaphore_signal(barrier, inc=1, device_id=(grid, (mem + o) % MEM), device_id_type=MESH)
    for d in (1, 3):
        pl.semaphore_signal(barrier, inc=1, device_id=at_z(d), device_id_type=MESH)

    for load in loads:
        load.wait()

    def to_stage(pair, parts):
        lanes = pl.ds(pl.multiple_of(pair * 128, 128), 128)
        for i in parts:
            block = (q_in, k_in, v_in)[i][:, lanes]
            if i == 0:
                block = block * bf16(0.125)
            block = block.T
            stage[pair * 2, pl.ds(i * HEAD, HEAD)] = block[:HEAD]
            stage[pair * 2 + 1, pl.ds(i * HEAD, HEAD)] = block[HEAD:]

    is_end = (p == 0) | (p == PLANE - 1)
    part_rows = (
        pl.ds(pl.multiple_of(jnp.where(is_end, HEAD, 0), HEAD), 2 * HEAD),
        pl.ds(pl.multiple_of(jnp.where(is_end, 0, 2 * HEAD), HEAD), HEAD),
    )

    def in_copy(dx, dy, part):
        target = ((x + dx) % 4) * 4 + (y + dy) % 4
        return pltpu.make_async_remote_copy(
            src_ref=stage.at[target, part_rows[part]],
            dst_ref=ext.at[1 + p, part_rows[part]],
            send_sem=in_send.at[part, dx * 4 + dy],
            recv_sem=in_recv.at[part, dx * 4 + dy],
            device_id=at_plane(x + dx, y + dy),
            device_id_type=MESH,
        )

    for dx in (0, 3, 2, 1):
        row = (x + dx) % 4
        to_stage(row * 2, (0, 1, 2))
        to_stage(row * 2 + 1, (0, 1, 2))
        if dx == 0:
            pl.semaphore_wait(barrier, 15 + 7 + 2)
        for a, b in offsets:
            if a == dx:
                in_copy(a, b, 0).start()

    ext[1 + p] = stage[p]

    load_truth.wait()

    def t_copy(dx, dy):
        return pltpu.make_async_remote_copy(
            src_ref=tstage.at[((x + dx) % 4) * 4 + (y + dy) % 4, own_rows],
            dst_ref=tgt.at[p],
            send_sem=t_send.at[dx * 4 + dy],
            recv_sem=t_recv.at[p],
            device_id=at_plane(x + dx, y + dy),
            device_id_type=MESH,
        )

    nodes = lax.broadcasted_iota(jnp.int32, (BLOCK, BLOCK), 0)
    pick = jnp.where(nodes == order[...], 1.0, 0.0).astype(bf16)
    for pair in range(8):
        ordered = dot(t_in[:, pair * 128 : pair * 128 + 128], pick, TN).astype(bf16)
        tstage[pair * 2] = ordered[:HEAD]
        tstage[pair * 2 + 1] = ordered[HEAD:]
    tgt[p] = tstage[p, own_rows]

    acc[...] = jnp.zeros_like(acc)
    for corner in ((pl.ds(0, BLOCK), pl.ds(BLOCK, BLOCK)), (pl.ds(5 * BLOCK, BLOCK), pl.ds(0, BLOCK))):
        for j in range(PLANE):
            weights[j, corner[0], corner[1]] = jnp.zeros((BLOCK, BLOCK), bf16)

    for dx, dy in offsets:
        in_copy(dx, dy, 0).wait_send()
    for dx, dy in offsets:
        in_copy(dx, dy, 1).start()
    for dx, dy in offsets:
        t_copy(dx, dy).start()

    far = jnp.where(widths[p] >= 2, 0.0, NEG).astype(f32)

    def halo_copy(up, part):
        src, dst = (PLANE, 0) if up else (1, PLANE + 1)
        i = (0 if up else 1) + 2 * part
        rows = pl.ds((1 + part) * HEAD, HEAD)
        return pltpu.make_async_remote_copy(
            src_ref=ext.at[src, rows],
            dst_ref=ext.at[dst, rows],
            send_sem=halo_send.at[i],
            recv_sem=halo_recv.at[i],
            device_id=at_z(1 if up else 3),
            device_id_type=MESH,
        )

    def natural(slot, part):
        (k_nat, v_nat)[part][slot] = ext[slot, pl.ds((1 + part) * HEAD, HEAD)].T

    def all_natural(part):
        def one(slot, carry):
            natural(slot, part)
            return carry

        lax.fori_loop(1, PLANE + 1, one, 0)

    def arrive(part):
        for dx, dy in offsets:
            in_copy(dx, dy, part).wait_recv()
        if part == 0:
            for up in (True, False):
                halo_copy(up, 0).start()
                halo_copy(up, 1).start()

    def arrive_halos(part):
        for up in (True, False):
            halo_copy(up, part).wait_recv()
        natural(0, part)
        natural(PLANE + 1, part)

    def unit_of(k):
        unit = (x + 1 + k) % 4
        return jnp.where(x == 2, 3 * k, unit) if k < 2 else jnp.where(x == 3, 5 - k, unit)

    def m1_copy(k, o):
        to = (mem + o) % MEM
        return pltpu.make_async_remote_copy(
            src_ref=out_u.at[k, to % 2, pl.ds(pl.multiple_of(to // 2 * SHARE, SHARE), SHARE)],
            dst_ref=ens.at[k, mem],
            send_sem=m1_send.at[k, o],
            recv_sem=m1_recv.at[k, o],
            device_id=(grid, (mem + o) % MEM),
            device_id_type=MESH,
        )

    def m2_copy(k, o):
        return pltpu.make_async_remote_copy(
            src_ref=gout.at[k, (mem + o) % MEM],
            dst_ref=g_u.at[k, core, own_rows],
            send_sem=m2_send.at[k, o],
            recv_sem=m2_recv.at[k, o],
            device_id=(grid, (mem + o) % MEM),
            device_id_type=MESH,
        )

    def lanes_of(i):
        return pl.ds(pl.multiple_of(i * BLOCK, BLOCK), BLOCK)

    def chunk_of(k, i):
        return (unit_of(k) * 4 + 1 + i) % PLANE

    def score(unit):
        def one(i, carry):
            j = (unit * 4 + 1 + i) % PLANE
            q_t = ext[j + 1, pl.ds(0, HEAD)]
            scores = [dot(k_nat[j + t], q_t, NN) for t in range(3)]
            for h in range(2):
                lanes = slice(h * BLOCK, h * BLOCK + BLOCK)
                tiles = []
                for n in range(5):
                    top = (h + n) % 2 * BLOCK
                    tiles.append(scores[(h + n) // 2][top : top + BLOCK, lanes])
                tiles[0] = tiles[0] + far
                tiles[4] = tiles[4] + far
                highest = functools.reduce(jnp.maximum, tiles)
                highest = jnp.max(highest, axis=0, keepdims=True)
                total = jnp.zeros((BLOCK, BLOCK), f32)
                for n in range(5):
                    term = jnp.exp(tiles[n] - highest)
                    total = total + term
                    weights[j, pl.ds((h + n) * BLOCK, BLOCK), lanes] = term.astype(bf16)
                share[j, :, lanes] = 1.0 / jnp.sum(total, axis=0, keepdims=True)
            return carry

        lax.fori_loop(0, 4, one, 0)

    def mix(k):
        if k == 1:
            arrive_halos(1)
        def one(i, carry):
            j = chunk_of(k, i)
            mixed = jnp.zeros((HEAD, CHUNK), f32)
            for t in range(3):
                mixed = mixed + dot(
                    ext[j + t, pl.ds(2 * HEAD, HEAD)], weights[j, pl.ds(t * CHUNK, CHUNK)], NN
                )
            mixed = (mixed * share[j]).astype(bf16)
            out_u[k, 0, :, lanes_of(i)] = mixed[:, :BLOCK]
            out_u[k, 1, :, lanes_of(i)] = mixed[:, BLOCK:]
            return carry

        lax.fori_loop(0, 4, one, 0)
        ens[k, mem] = out_u[k, core, own_rows]

    def m1_start(k):
        if k > 0:
            for o in range(1, MEM):
                m1_copy(k - 1, o).wait_send()
        for o in (1, 7, 2, 6, 3, 5, 4):
            m1_copy(k, o).start()

    def truth_arrive(k):
        for i in range(4):
            j = chunk_of(k, i)

            @pl.when(j != p)
            def _():
                pltpu.make_async_remote_copy(
                    src_ref=tstage.at[0, own_rows],
                    dst_ref=tgt.at[j],
                    send_sem=t_send.at[0],
                    recv_sem=t_recv.at[j],
                    device_id=(z_hi * 16 + j, mem),
                    device_id_type=MESH,
                ).wait_recv()

    def crps(k):
        truth_arrive(k)
        for o in range(1, MEM):
            m1_copy(k, o).wait_recv()
        own = [ens[k, n].astype(f32) for n in range(MEM)]
        target = jnp.concatenate([tgt[chunk_of(k, i)] for i in range(4)], axis=1).astype(f32)
        totals = [jnp.zeros((SHARE, UNITS * BLOCK), f32) for _ in range(MEM)]
        for a in range(MEM):
            for b in range(a + 1, MEM):
                s = slope(own[a] - own[b])
                totals[a] = totals[a] + s
                totals[b] = totals[b] - s
        for n in range(MEM):
            gout[k, n] = (slope(own[n] - target) - totals[n] * (1.0 / (MEM - 1))).astype(bf16)
        for o in (1, 7, 2, 6, 3, 5, 4):
            m2_copy(k, o).start()
        g_u[k, core, own_rows] = gout[k, mem]

    def dq_copy(j):
        return pltpu.make_async_remote_copy(
            src_ref=dq_src.at[j],
            dst_ref=dq_dst.at[p],
            send_sem=dq_send.at[j],
            recv_sem=dq_recv.at[p],
            device_id=(z_hi * 16 + j, mem),
            device_id_type=MESH,
        )

    def dkv_copy(j):
        return pltpu.make_async_remote_copy(
            src_ref=dkv_src.at[j],
            dst_ref=dkv_dst.at[p],
            send_sem=dkv_send.at[j],
            recv_sem=dkv_recv.at[p],
            device_id=(z_hi * 16 + j, mem),
            device_id_type=MESH,
        )

    def back_copy(down):
        i = 0 if down else 1
        return pltpu.make_async_remote_copy(
            src_ref=dkv_src.at[PLANE + i],
            dst_ref=(back_high if down else back_low),
            send_sem=back_send.at[i],
            recv_sem=back_recv.at[i],
            device_id=at_z(3 if down else 1),
            device_id_type=MESH,
        )

    def finish_dkv(j):
        dkv_src[j] = acc[j + 1].astype(bf16)

        @pl.when(j != p)
        def _():
            dkv_copy(j).start()

        @pl.when(j == p)
        def _():
            dkv_dst[p] = dkv_src[p]

    def finish_ends():
        back_copy(True).wait_recv()
        acc[PLANE] += back_high[...].astype(f32)
        finish_dkv(PLANE - 1)
        back_copy(False).wait_recv()
        acc[1] += back_low[...].astype(f32)
        finish_dkv(0)

    left = lax.broadcasted_iota(jnp.int32, (CHUNK, 2 * HEAD), 1) < HEAD

    def backward(k):
        for o in range(1, MEM):
            m2_copy(k, o).wait_recv()

        def one(i):
            j = chunk_of(k, i)
            g_t = jnp.concatenate([g_u[k, c, :, lanes_of(i)] for c in range(2)], axis=1).astype(f32)
            o_t = jnp.concatenate([out_u[k, c, :, lanes_of(i)] for c in range(2)], axis=1).astype(f32)
            scale = share[j]
            inner = jnp.sum(g_t * o_t, axis=0, keepdims=True) * scale
            g_t = (g_t * scale).astype(bf16)
            both = jnp.concatenate([ext[j + 1, pl.ds(0, HEAD)], g_t], axis=0).T
            q_side = jnp.where(left, both, bf16(0))
            g_side = jnp.where(left, bf16(0), both)
            dq = jnp.zeros((HEAD, CHUNK), f32)
            for t in range(3):
                along = dot(v_nat[j + t], g_t, NN)
                low = weights[j, pl.ds(t * CHUNK, CHUNK)]
                ds = (low.astype(f32) * (along - inner)).astype(bf16)
                dq = dq + dot(ext[j + t, pl.ds(HEAD, HEAD)], ds, NN)
                acc[j + t] += dot(ds, q_side, NN) + dot(low, g_side, NN)
            dq_src[j] = (dq * 0.125).astype(bf16)

            @pl.when(j != p)
            def _():
                dq_copy(j).start()

            @pl.when(j == p)
            def _():
                dq_dst[p] = dq_src[p]

        def ends(n, carry):
            one(3 - n)
            return carry

        lax.fori_loop(0, 2, ends, 0)

        @pl.when(unit_of(k) == 3)
        def _():
            dkv_src[PLANE] = acc[0].astype(bf16)
            back_copy(True).start()
            dkv_src[PLANE + 1] = acc[PLANE + 1].astype(bf16)
            back_copy(False).start()

        def others(i, carry):
            one(i)
            return carry

        lax.fori_loop(0, 2, others, 0)

        def done(i, carry):
            j = (unit_of(k) * 4 + i) % PLANE

            @pl.when((j != 0) & (j != PLANE - 1))
            def _():
                finish_dkv(j)

            return carry

        if k in (1, 2):

            @pl.when(x == k + 1)
            def _():
                finish_dkv(PLANE - 2)
                finish_dkv(1)

            @pl.when(x != k + 1)
            def _():
                lax.fori_loop(0, 4, done, 0)
        else:
            lax.fori_loop(2 if k == 0 else 0, 6 if k == UNITS - 1 else 4, done, 0)
        if k == 2:
            pl.when((x == 1) | (x == 2))(finish_ends)
        if k == 3:
            pl.when((x == 0) | (x == 3))(finish_ends)

    arrive(0)
    all_natural(0)
    for unit in range(3):
        score(unit)
    arrive(1)
    mix(0)
    m1_start(0)
    arrive_halos(0)
    score(3)
    mix(1)
    mix(2)
    mix(3)
    m1_start(1)
    all_natural(1)
    crps(0)
    m1_start(2)
    crps(1)
    m1_start(3)
    backward(0)
    crps(2)
    backward(1)
    crps(3)
    backward(2)
    backward(3)

    def all_arrived(ref, recv):
        def one(n, carry):
            src = (p + n) % PLANE
            pltpu.make_async_remote_copy(
                src_ref=ref.at[src], dst_ref=ref.at[src], send_sem=dq_send.at[0], recv_sem=recv.at[src],
                device_id=(z_hi * 16 + src, mem), device_id_type=MESH,
            ).wait_recv()
            return carry

        lax.fori_loop(1, PLANE, one, 0)

    all_arrived(dq_dst, dq_recv)
    all_arrived(dkv_dst, dkv_recv)
    for dx, dy in offsets:
        in_copy(dx, dy, 1).wait_send()
    for up in (True, False):
        for part in range(2):
            halo_copy(up, part).wait_send()
        back_copy(up).wait_send()
    for o in range(1, MEM):
        m1_copy(UNITS - 1, o).wait_send()
        for k in range(UNITS):
            m2_copy(k, o).wait_send()

    for dx, dy in offsets:
        t_copy(dx, dy).wait_send()

    def sent(n, carry):
        j = (p + n) % PLANE
        dq_copy(j).wait_send()
        dkv_copy(j).wait_send()
        return carry

    lax.fori_loop(1, PLANE, sent, 0)


def assemble(dq, dkv, dq_out, dk_out, dv_out):
    for pair in range(dq.shape[0] // 2):
        lanes = slice(pair * 128, pair * 128 + 128)
        dq_out[0, :, lanes] = jnp.concatenate([dq[2 * pair], dq[2 * pair + 1]], axis=0).T
        even, odd = dkv[2 * pair], dkv[2 * pair + 1]
        dk_out[0, :, lanes] = jnp.concatenate([even[:, :HEAD], odd[:, :HEAD]], axis=1)
        dv_out[0, :, lanes] = jnp.concatenate([even[:, HEAD:], odd[:, HEAD:]], axis=1)


def on_device(queries, keys, values, truth, widths, node_order):
    bf16 = jnp.bfloat16
    shape = queries.shape
    dma = pltpu.SemaphoreType.DMA
    vmem = pltpu.VMEM
    dq, dkv = pl.pallas_call(
        kernel,
        out_shape=[
            jax.ShapeDtypeStruct((PLANE, HEAD, CHUNK), bf16),
            jax.ShapeDtypeStruct((PLANE, CHUNK, 2 * HEAD), bf16),
        ],
        in_specs=[
            pl.BlockSpec(memory_space=pltpu.SMEM),
            pl.BlockSpec(memory_space=pltpu.VMEM),
        ]
        + [pl.BlockSpec(memory_space=pl.ANY)] * 4,
        out_specs=[pl.BlockSpec(memory_space=pltpu.VMEM)] * 2,
        scratch_shapes=[
            vmem((256, 1024), bf16),
            vmem((256, 1024), bf16),
            vmem((256, 1024), bf16),
            vmem((128, 1024), bf16),
            vmem((PLANE, 3 * HEAD, CHUNK), bf16),
            vmem((PLANE + 2, 3 * HEAD, CHUNK), bf16),
            vmem((PLANE + 2, CHUNK, HEAD), bf16),
            vmem((PLANE + 2, CHUNK, HEAD), bf16),
            vmem((PLANE, HEAD, BLOCK), bf16),
            vmem((PLANE, SHARE, BLOCK), bf16),
            vmem((PLANE, 3 * CHUNK, CHUNK), bf16),
            vmem((PLANE, 1, CHUNK), jnp.float32),
            vmem((UNITS, 2, HEAD, 4 * BLOCK), bf16),
            vmem((UNITS, MEM, SHARE, 4 * BLOCK), bf16),
            vmem((UNITS, MEM, SHARE, 4 * BLOCK), bf16),
            vmem((UNITS, 2, HEAD, 4 * BLOCK), bf16),
            vmem((PLANE + 2, CHUNK, 2 * HEAD), jnp.float32),
            vmem((CHUNK, 2 * HEAD), bf16),
            vmem((CHUNK, 2 * HEAD), bf16),
            vmem((PLANE, HEAD, CHUNK), bf16),
            vmem((PLANE + 2, CHUNK, 2 * HEAD), bf16),
            dma((4,)),
            dma((2, 16)),
            dma((2, 16)),
            dma((16,)),
            dma((16,)),
            dma((4,)),
            dma((4,)),
            dma((UNITS, MEM)),
            dma((UNITS, MEM)),
            dma((UNITS, MEM)),
            dma((UNITS, MEM)),
            dma((2,)),
            dma((2,)),
            dma((PLANE,)),
            dma((PLANE,)),
            dma((PLANE,)),
            dma((PLANE,)),
        ],
        compiler_params=pltpu.CompilerParams(
            collective_id=0, has_side_effects=True, vmem_limit_bytes=62 << 20
        ),
        name="band_attention",
    )(widths, node_order.reshape(1, BLOCK), queries, keys, values, truth)
    steps = 4
    heads = PLANE // steps
    return pl.pallas_call(
        assemble,
        grid=(steps,),
        out_shape=[jax.ShapeDtypeStruct(shape, bf16)] * 3,
        in_specs=[
            pl.BlockSpec((heads, HEAD, CHUNK), lambda i: (i, 0, 0)),
            pl.BlockSpec((heads, CHUNK, 2 * HEAD), lambda i: (i, 0, 0)),
        ],
        out_specs=[pl.BlockSpec((1, CHUNK, heads * HEAD), lambda i: (0, 0, i))] * 3,
        name="assemble",
    )(dq, dkv)


def solution(mesh):
    placed = (
        P("mem", "grid", None),
        P("mem", "grid", None),
        P("mem", "grid", None),
        P("grid", None),
        P(),
        P(),
    )
    return jax.shard_map(
        on_device,
        mesh=mesh,
        in_specs=placed,
        out_specs=(P("mem", "grid", None), P("mem", "grid", None), P("mem", "grid", None)),
        check_vma=False,
    )
```
